32 devices in a mesh: patch: 4 (over z), tm: 2 (over y), subject: 4 (over x, core).
Axes of the slice: x: 2, y: 2, z: 4, core: 2. Of those that a mesh axis runs over, the one named last changes fastest.
Arguments:
- frames_in: bfloat16 [32, 512, 512], P(('subject', 'patch', 'tm')), parts along dimension 0, may hold values from -6 to 6
- spatial_qkv: bfloat16 [512, 1536], replicated, may hold values from -20 to 20, as said below
- spatial_out: bfloat16 [512, 512], replicated, may hold values from -0.25 to 0.25
- temporal_qkv: bfloat16 [512, 1536], replicated, may hold values from -20 to 20, as said below
- temporal_out: bfloat16 [512, 512], replicated, may hold values from -0.25 to 0.25
Outputs:
- frames_out: bfloat16 [32, 512, 512], P(('subject', 'patch', 'tm')), parts along dimension 0
The draws below stay inside these ranges and needn't reach their ends.
There are 4 independent parts, one for each index of `subject`. The reference program is written for one: setup_inputs(seed, part) draws one part's arguments, and reference() takes and returns one part's arrays. A program takes and returns all parts, laid end to end along the dimension named above; an argument that names none is the same for every part. Nothing has to cross between parts.
Inputs may be any that keep to these rules, and one draw needn't show every extreme that they name: `spatial_qkv`: columns hold query, key and value projections in that order, each 8 heads of 64. `temporal_qkv`: columns hold query, key and value projections in that order, each 8 heads of 64.
All inputs are finite; a program needn't handle non-finite values.
Results may differ from the reference program's by a relative error of at most 0.015.
Values may be sent and summed in bfloat16 or wider, within the bound.
A program may use at most 64 MiB of HBM per device.

```python
import jax
import jax.numpy as jnp
from jax import lax

D = 512
HEADS = 8
PATCHES = 512
FRAMES = 8


def qkv_table(key):
    split_query, split_keys, split_values = jax.random.split(key, 3)
    spread = D ** (-0.5)
    queries = jax.random.normal(split_query, (D, D), jnp.float32) * (1.4 * spread)
    key_part = jax.random.normal(split_keys, (D, D), jnp.float32) * (1.4 * spread)
    value_part = jax.random.normal(split_values, (D, D), jnp.float32) * (2.0 * spread)
    return jnp.concatenate([queries, key_part, value_part], axis=1)


def draw_spatial_qkv(key, part):
    return qkv_table(jax.random.fold_in(key, 11)).astype(jnp.bfloat16)


def draw_temporal_qkv(key, part):
    return qkv_table(jax.random.fold_in(key, 23)).astype(jnp.bfloat16)


def levels(own_key, shape, cuts, low, high):
    def one(dim, blocks):
        draws = jax.random.uniform(jax.random.fold_in(jax.random.fold_in(own_key, 6), dim), (blocks,), jnp.float32, low / len(cuts), high / len(cuts))
        return jnp.repeat(jnp.exp(draws), shape[dim] // blocks).reshape((-1,) + (1,) * (len(shape) - dim - 1))

    factor_of = one(*cuts[0])
    for cut in cuts[1:]:
        factor_of = factor_of * one(*cut)
    return factor_of


def normal_values(rng, dims, width, bound, shards=(), held_as=jnp.bfloat16):
    values = jax.random.normal(rng, dims, jnp.float32) * width
    if len(shards) > 0:
        values = levels(rng, dims, shards, -0.22, 0.18) * values
    return jnp.clip(values, min=-bound, max=bound).astype(held_as)


def setup_inputs(seed: int = 0, part: int = 0) -> dict:
    seeds = jax.random.split(jax.random.key(seed), 6)
    own_keys = jax.random.split(jax.random.fold_in(seeds[5], part), 6)
    return {
        "frames_in": normal_values(own_keys[0], (FRAMES, PATCHES, D), 1.0, 6.0, ((0, 8),)),
        "spatial_qkv": draw_spatial_qkv(jax.random.fold_in(seeds[5], 71), part),
        "spatial_out": normal_values(seeds[2], (D, D), D ** -0.5, 0.25),
        "temporal_qkv": draw_temporal_qkv(jax.random.fold_in(seeds[5], 71), part),
        "temporal_out": normal_values(seeds[4], (D, D), D ** -0.5, 0.25),
    }


epsilon = 1e-05
floor_score = -1e+30

def layer_norm(input_rows):
    as_float = input_rows.astype(jnp.float32)
    centre = lax.optimization_barrier(jnp.mean(as_float, axis=-1, keepdims=True))
    centered = as_float - centre
    spread = lax.optimization_barrier(jnp.mean(centered * centered, axis=-1, keepdims=True))
    return (centered * lax.rsqrt(spread + epsilon)).astype(jnp.bfloat16)

def project_heads(input_rows, qkv_weight):
    model_width = input_rows.shape[-1]
    normed = layer_norm(input_rows)
    packed = jnp.dot(normed.reshape(-1, model_width), qkv_weight, preferred_element_type=jnp.float32).astype(jnp.bfloat16)
    packed = lax.optimization_barrier(packed).astype(jnp.float32)
    shaped = packed.reshape(input_rows.shape[:-1] + (3, HEADS, model_width // HEADS))
    return (shaped[..., 0, :, :], shaped[..., 1, :, :], shaped[..., 2, :, :])

def spatial_frame(one_frame, qkv_weight, out_weight):
    queries, key_rows, value_rows = project_heads(one_frame, qkv_weight)
    factor = queries.shape[-1] ** (-0.5)
    scores = jnp.einsum('qhd,khd->hqk', queries, key_rows) * factor
    highest = lax.optimization_barrier(jnp.max(scores, axis=-1, keepdims=True))
    exp_terms = jnp.exp(scores - highest)
    row_total = lax.optimization_barrier(jnp.sum(exp_terms, axis=-1))
    weights = lax.optimization_barrier(exp_terms.astype(jnp.bfloat16)).astype(jnp.float32)
    mixture = jnp.einsum('hqk,khd->qhd', weights, value_rows)
    mixture = (mixture / jnp.transpose(row_total)[:, :, None]).astype(jnp.bfloat16)
    update = jnp.dot(mixture.reshape(one_frame.shape), out_weight, preferred_element_type=jnp.float32)
    return (one_frame.astype(jnp.float32) + update).astype(jnp.bfloat16)

def causal_columns(columns, qkv_weight, out_weight):
    queries, key_rows, value_rows = project_heads(columns, qkv_weight)
    factor = queries.shape[-1] ** (-0.5)
    scores = jnp.einsum('qchd,kchd->chqk', queries, key_rows) * factor
    frame_order = jnp.arange(columns.shape[0], dtype=jnp.int32)
    allowed = frame_order[None, :] <= frame_order[:, None]
    masked = jnp.where(allowed, scores, floor_score)
    highest = lax.optimization_barrier(jnp.max(masked, axis=-1, keepdims=True))
    exp_terms = jnp.where(allowed, jnp.exp(masked - highest), 0.0)
    row_total = lax.optimization_barrier(jnp.sum(exp_terms, axis=-1))
    weights = lax.optimization_barrier(exp_terms.astype(jnp.bfloat16)).astype(jnp.float32)
    mixture = jnp.einsum('chqk,kchd->qchd', weights, value_rows)
    mixture = (mixture / jnp.transpose(row_total, (2, 0, 1))[..., None]).astype(jnp.bfloat16)
    model_width = columns.shape[-1]
    update = jnp.dot(mixture.reshape(-1, model_width), out_weight, preferred_element_type=jnp.float32)
    return (columns.astype(jnp.float32) + update.reshape(columns.shape)).astype(jnp.bfloat16)

def reference(frames_in, spatial_qkv, spatial_out, temporal_qkv, temporal_out):

    def frame_step(one_frame):
        return spatial_frame(one_frame, spatial_qkv, spatial_out)
    hidden = lax.map(frame_step, frames_in)
    group_size = 8
    grouped = hidden.reshape(FRAMES, PATCHES // group_size, group_size, D).transpose(1, 0, 2, 3)

    def group_step(columns):
        return causal_columns(columns, temporal_qkv, temporal_out)
    result = lax.map(group_step, grouped)
    return result.transpose(1, 0, 2, 3).reshape(FRAMES, PATCHES, D)
```

```python
import functools

import jax
import jax.numpy as jnp
from jax import lax
from jax.experimental import pallas as pl
from jax.experimental.pallas import tpu as pltpu
from jax.sharding import PartitionSpec as P

HEADS = 8
PAIR = 128
CHUNKS = 2

epsilon = 1e-05
floor_score = -1e30
MESH = pl.DeviceIdType.MESH
bf16, f32 = jnp.bfloat16, jnp.float32


def layer_norm(input_rows):
    as_float = input_rows.astype(f32)
    centre = jnp.mean(as_float, axis=-1, keepdims=True)
    centered = as_float - centre
    spread = jnp.mean(centered * centered, axis=-1, keepdims=True)
    return (centered * lax.rsqrt(spread + epsilon)).astype(bf16)


def dot(a, b):
    return jnp.dot(a, b, preferred_element_type=f32)


def dot_t(a, b):
    return lax.dot_general(a, b, (((1,), (1,)), ((), ())), preferred_element_type=f32)


def stacked_heads(q_pair, low):
    zero = jnp.zeros_like(q_pair)
    return jnp.concatenate([jnp.where(low, q_pair, zero), jnp.where(low, zero, q_pair)], axis=0)


def attend(q_pair, k_pair, v_pair, allowed):
    rows, keys = q_pair.shape[0], k_pair.shape[0]
    low = lax.broadcasted_iota(jnp.int32, (rows, PAIR), 1) < PAIR // 2
    scores = dot_t(stacked_heads(q_pair, low), k_pair)
    if allowed is not None:
        scores = jnp.where(allowed, scores, floor_score)
    highest = jnp.max(scores, axis=-1, keepdims=True)
    exp_terms = jnp.exp(scores - highest)
    if allowed is not None:
        exp_terms = jnp.where(allowed, exp_terms, 0.0)
    values = jnp.concatenate([v_pair, jnp.ones((keys, PAIR), bf16)], axis=1)
    mixed = dot(exp_terms.astype(bf16), values)
    mixed = mixed[:, :PAIR] / mixed[:, PAIR:]
    return jnp.where(low, mixed[:rows], mixed[rows:]).astype(bf16)


def fused_kernel(zs, ys, x_hbm, sqkv_hbm, sout_hbm, tqkv_hbm, tout_hbm, out_ref,
                 x, sqkv, sout, tqkv, tout, packed, hid, recv, tpacked, attn, tattn, res,
                 load_sem, own_sem, fsend, frecv, bsend, brecv):
    patches, width = x.shape
    group = zs * ys
    block = patches // group
    part = block // CHUNKS
    z, y = lax.axis_index("patch"), lax.axis_index("tm")
    me = z * ys + y
    half = zs // 2
    pairs = width // PAIR
    scale = (width // HEADS) ** -0.5

    order = []
    for j in range(zs):
        base = (z // half) * half
        if j < half:
            base = half - base
        zz = base + (z % half + j % half + (1 if j >= half else 0)) % half
        for i in range(ys):
            yy = (y + i + 1) % ys
            order.append((zz, yy, zz * ys + yy))
    peers = order[:-1]

    barrier = pltpu.get_barrier_semaphore()
    for zz, yy, _ in peers:
        pl.semaphore_signal(barrier, inc=1, device_id={"patch": zz, "tm": yy}, device_id_type=MESH)
    loads = [
        pltpu.make_async_copy(src, dst, load_sem.at[i])
        for i, (src, dst) in enumerate(
            [(x_hbm, x), (sqkv_hbm, sqkv), (sout_hbm, sout), (tqkv_hbm, tqkv), (tout_hbm, tout)]
        )
    ]
    for copy in loads:
        copy.start()

    def rows_of(d, c):
        return pl.ds(pl.multiple_of(d * block + c * part, 16), part)

    def forward(zz, yy, d, c):
        return pltpu.make_async_remote_copy(
            src_ref=hid.at[rows_of(d, c)], dst_ref=recv.at[c, me],
            send_sem=fsend.at[c, d], recv_sem=frecv.at[c, me],
            device_id={"patch": zz, "tm": yy}, device_id_type=MESH)

    def forward_in(zz, yy, d, c):
        return pltpu.make_async_remote_copy(
            src_ref=hid.at[rows_of(d, c)], dst_ref=recv.at[c, d],
            send_sem=fsend.at[c, d], recv_sem=frecv.at[c, d],
            device_id={"patch": zz, "tm": yy}, device_id_type=MESH)

    def back(zz, yy, d, c):
        return pltpu.make_async_remote_copy(
            src_ref=res.at[c, d], dst_ref=out_ref.at[rows_of(me, c)],
            send_sem=bsend.at[c, d], recv_sem=brecv.at[c, me],
            device_id={"patch": zz, "tm": yy}, device_id_type=MESH)

    def back_in(zz, yy, d, c):
        return pltpu.make_async_remote_copy(
            src_ref=res.at[c, d], dst_ref=out_ref.at[rows_of(d, c)],
            send_sem=bsend.at[c, d], recv_sem=brecv.at[c, d],
            device_id={"patch": zz, "tm": yy}, device_id_type=MESH)

    loads[0].wait()
    loads[1].wait()
    normed = layer_norm(x[...])
    packed[:, :width] = (dot(normed, sqkv[:, :width]).astype(bf16) * scale).astype(bf16)
    packed[:, width:] = dot(normed, sqkv[:, width:]).astype(bf16)
    loads[2].wait()
    pl.semaphore_wait(barrier, group - 1)

    for j in range(zs):
        zz = order[j * ys][0]
        rows = pl.ds(pl.multiple_of(zz * (ys * block), ys * block), ys * block)
        for p in range(pairs):
            lanes = slice(p * PAIR, (p + 1) * PAIR)
            attn[:, lanes] = attend(
                packed[rows, p * PAIR:(p + 1) * PAIR],
                packed[:, width + p * PAIR:width + (p + 1) * PAIR],
                packed[:, 2 * width + p * PAIR:2 * width + (p + 1) * PAIR], None)
        hid[rows, :] = (x[rows, :].astype(f32) + dot(attn[...], sout[...])).astype(bf16)
        for i in range(ys):
            zz, yy, d = order[j * ys + i]
            if j * ys + i < group - 1:
                forward(zz, yy, d, 0).start()
    for zz, yy, d in peers:
        for c in range(1, CHUNKS):
            forward(zz, yy, d, c).start()
    for c in range(CHUNKS):
        recv[c, pl.ds(me, 1)] = hid[rows_of(me, c), :].reshape(1, part, width)
    loads[3].wait()
    loads[4].wait()

    sub = 16
    keys = group * sub
    at_q = lax.broadcasted_iota(jnp.int32, (2 * keys, keys), 0) % keys
    at_k = lax.broadcasted_iota(jnp.int32, (2 * keys, keys), 1)
    allowed = (at_q % sub == at_k % sub) & (at_k // sub <= at_q // sub)
    for c in range(CHUNKS):
        for zz, yy, d in peers:
            forward_in(zz, yy, d, c).wait_recv()
        got = recv[c].reshape(group * part, width)
        normed = layer_norm(got)
        tpacked[:, :, :width] = (
            (dot(normed, tqkv[:, :width]).astype(bf16) * scale).astype(bf16).reshape(group, part, width))
        tpacked[:, :, width:] = (
            dot(normed, tqkv[:, width:]).astype(bf16).reshape(group, part, 2 * width))
        for s in range(part // sub):
            at = slice(s * sub, (s + 1) * sub)
            for p in range(pairs):
                lanes = slice(p * PAIR, (p + 1) * PAIR)
                q, k, v = (
                    tpacked[:, at, w * width + p * PAIR:w * width + (p + 1) * PAIR].reshape(keys, PAIR)
                    for w in range(3)
                )
                tattn[:, at, lanes] = attend(q, k, v, allowed).reshape(group, sub, PAIR)
        update = dot(tattn[...].reshape(group * part, width), tout[...])
        res[c] = (got.astype(f32) + update).astype(bf16).reshape(group, part, width)
        for zz, yy, d in peers:
            back(zz, yy, d, c).start()
        pltpu.make_async_copy(res.at[c, me], out_ref.at[rows_of(me, c)], own_sem.at[c]).start()

    for c in range(CHUNKS):
        for zz, yy, d in peers:
            forward(zz, yy, d, c).wait_send()
            back(zz, yy, d, c).wait_send()
            back_in(zz, yy, d, c).wait_recv()
        pltpu.make_async_copy(res.at[c, me], out_ref.at[rows_of(me, c)], own_sem.at[c]).wait()


def fused(zs, ys, frame, sqkv, sout, tqkv, tout):
    patches, width = frame.shape
    group = zs * ys
    block = patches // group
    part = block // CHUNKS
    anywhere = pl.BlockSpec(memory_space=pl.ANY)
    dma = pltpu.SemaphoreType.DMA
    return pl.pallas_call(
        functools.partial(fused_kernel, zs, ys),
        out_shape=jax.ShapeDtypeStruct((patches, width), bf16),
        in_specs=[anywhere] * 5,
        out_specs=anywhere,
        scratch_shapes=[
            pltpu.VMEM((patches, width), bf16),
            pltpu.VMEM(sqkv.shape, bf16),
            pltpu.VMEM(sout.shape, bf16),
            pltpu.VMEM(tqkv.shape, bf16),
            pltpu.VMEM(tout.shape, bf16),
            pltpu.VMEM((patches, 3 * width), bf16),
            pltpu.VMEM((patches, width), bf16),
            pltpu.VMEM((CHUNKS, group, part, width), bf16),
            pltpu.VMEM((group, part, 3 * width), bf16),
            pltpu.VMEM((ys * block, width), bf16),
            pltpu.VMEM((group, part, width), bf16),
            pltpu.VMEM((CHUNKS, group, part, width), bf16),
            dma((5,)),
            dma((CHUNKS,)),
            dma((CHUNKS, group)),
            dma((CHUNKS, group)),
            dma((CHUNKS, group)),
            dma((CHUNKS, group)),
        ],
        compiler_params=pltpu.CompilerParams(
            collective_id=0, has_side_effects=True, vmem_limit_bytes=48 * 2**20),
    )(frame, sqkv, sout, tqkv, tout)


def spatial_frame(one_frame, qkv_weight, out_weight):
    width = one_frame.shape[-1]
    scale = (width // HEADS) ** -0.5
    packed = dot(layer_norm(one_frame), qkv_weight).astype(bf16)
    queries, keys, values = jnp.split(packed, 3, axis=-1)
    queries = (queries * scale).astype(bf16)
    mixture = jnp.concatenate(
        [attend(queries[:, a:a + PAIR], keys[:, a:a + PAIR], values[:, a:a + PAIR], None)
         for a in range(0, width, PAIR)], axis=-1)
    return (one_frame.astype(f32) + dot(mixture, out_weight)).astype(bf16)


def temporal_columns(columns, qkv_weight, out_weight):
    frames, count, width = columns.shape
    scale = (width // HEADS) ** -0.5
    rows = columns.reshape(frames * count, width)
    packed = dot(layer_norm(rows), qkv_weight).astype(bf16)
    queries, keys, values = jnp.split(packed, 3, axis=-1)
    queries = (queries * scale).astype(bf16)
    place = jnp.arange(frames * count, dtype=jnp.int32)
    allowed = (place[:, None] % count == place[None, :] % count) & (
        place[None, :] // count <= place[:, None] // count)
    allowed = jnp.concatenate([allowed, allowed], axis=0)
    mixture = jnp.concatenate(
        [attend(queries[:, a:a + PAIR], keys[:, a:a + PAIR], values[:, a:a + PAIR], allowed)
         for a in range(0, width, PAIR)], axis=-1)
    return (rows.astype(f32) + dot(mixture, out_weight)).astype(bf16).reshape(columns.shape)


def solution(mesh):
    zs, ys = mesh.shape["patch"], mesh.shape["tm"]
    group = zs * ys

    def body(frames_in, spatial_qkv, spatial_out, temporal_qkv, temporal_out):
        frames, patches, width = frames_in.shape
        if frames == 1 and zs % 2 == 0 and patches % (16 * CHUNKS * group) == 0:
            return fused(zs, ys, frames_in[0], spatial_qkv, spatial_out, temporal_qkv, temporal_out)[None]
        hidden = lax.map(lambda frame: spatial_frame(frame, spatial_qkv, spatial_out), frames_in)
        columns = lax.all_to_all(hidden, ("patch", "tm"), split_axis=1, concat_axis=0, tiled=True)
        result = temporal_columns(columns, temporal_qkv, temporal_out)
        return lax.all_to_all(result, ("patch", "tm"), split_axis=0, concat_axis=1, tiled=True)

    in_specs = (P(("subject", "patch", "tm"), None, None), P(), P(), P(), P())
    out_specs = P(("subject", "patch", "tm"), None, None)
    return jax.shard_map(body, mesh=mesh, in_specs=in_specs, out_specs=out_specs, check_vma=False)
```

```python
import functools

import jax
import jax.numpy as jnp
from jax import lax
from jax.experimental import pallas as pl
from jax.experimental.pallas import tpu as pltpu
from jax.sharding import PartitionSpec as P

HEADS = 8
PAIR = 128
CHUNKS = 2

epsilon = 1e-05
floor_score = -1e30
MESH = pl.DeviceIdType.MESH
bf16, f32 = jnp.bfloat16, jnp.float32


def layer_norm(input_rows):
    as_float = input_rows.astype(f32)
    centre = jnp.mean(as_float, axis=-1, keepdims=True)
    centered = as_float - centre
    spread = jnp.mean(centered * centered, axis=-1, keepdims=True)
    return (centered * lax.rsqrt(spread + epsilon)).astype(bf16)


def dot(a, b):
    return jnp.dot(a, b, preferred_element_type=f32)


def dot_t(a, b):
    return lax.dot_general(a, b, (((1,), (1,)), ((), ())), preferred_element_type=f32)


def stacked_heads(q_pair, low):
    zero = jnp.zeros_like(q_pair)
    return jnp.concatenate([jnp.where(low, q_pair, zero), jnp.where(low, zero, q_pair)], axis=0)


def attend(q_pair, k_pair, v_pair, allowed):
    rows, keys = q_pair.shape[0], k_pair.shape[0]
    low = lax.broadcasted_iota(jnp.int32, (rows, PAIR), 1) < PAIR // 2
    scores = dot_t(stacked_heads(q_pair, low), k_pair)
    if allowed is not None:
        scores = jnp.where(allowed, scores, floor_score)
    highest = jnp.max(scores, axis=-1, keepdims=True)
    exp_terms = jnp.exp(scores - highest)
    if allowed is not None:
        exp_terms = jnp.where(allowed, exp_terms, 0.0)
    values = jnp.concatenate([v_pair, jnp.ones((keys, PAIR), bf16)], axis=1)
    mixed = dot(exp_terms.astype(bf16), values)
    mixed = mixed[:, :PAIR] / mixed[:, PAIR:]
    return jnp.where(low, mixed[:rows], mixed[rows:]).astype(bf16)


def fused_kernel(zs, ys, x_hbm, sqkv_hbm, sout_hbm, tqkv_hbm, tout_hbm, out_ref,
                 x, sqkv, sout, tqkv, tout, packed, hid, recv, tpacked, attn, tattn, res,
                 load_sem, own_sem, fsend, frecv, bsend, brecv):
    patches, width = x.shape
    group = zs * ys
    block = patches // group
    part = block // CHUNKS
    z, y = lax.axis_index("patch"), lax.axis_index("tm")
    me = z * ys + y
    half = zs // 2
    pairs = width // PAIR
    scale = (width // HEADS) ** -0.5

    order = []
    for j in range(zs):
        base = (z // half) * half
        if j < half:
            base = half - base
        zz = base + (z % half + j % half + (1 if j >= half else 0)) % half
        for i in range(ys):
            yy = (y + i + 1) % ys
            order.append((zz, yy, zz * ys + yy))
    peers = order[:-1]

    barrier = pltpu.get_barrier_semaphore()
    for zz, yy, _ in peers:
        pl.semaphore_signal(barrier, inc=1, device_id={"patch": zz, "tm": yy}, device_id_type=MESH)
    loads = [
        pltpu.make_async_copy(src, dst, load_sem.at[i])
        for i, (src, dst) in enumerate(
            [(x_hbm, x), (sqkv_hbm, sqkv), (sout_hbm, sout), (tqkv_hbm, tqkv), (tout_hbm, tout)]
        )
    ]
    for copy in loads:
        copy.start()

    def rows_of(d, c):
        return pl.ds(pl.multiple_of(d * block + c * part, 16), part)

    def forward(zz, yy, d, c):
        return pltpu.make_async_remote_copy(
            src_ref=hid.at[rows_of(d, c)], dst_ref=recv.at[c, me],
            send_sem=fsend.at[c, d], recv_sem=frecv.at[c, me],
            device_id={"patch": zz, "tm": yy}, device_id_type=MESH)

    def forward_in(zz, yy, d, c):
        return pltpu.make_async_remote_copy(
            src_ref=hid.at[rows_of(d, c)], dst_ref=recv.at[c, d],
            send_sem=fsend.at[c, d], recv_sem=frecv.at[c, d],
            device_id={"patch": zz, "tm": yy}, device_id_type=MESH)

    def back(zz, yy, d, c):
        return pltpu.make_async_remote_copy(
            src_ref=res.at[c, d], dst_ref=out_ref.at[rows_of(me, c)],
            send_sem=bsend.at[c, d], recv_sem=brecv.at[c, me],
            device_id={"patch": zz, "tm": yy}, device_id_type=MESH)

    def back_in(zz, yy, d, c):
        return pltpu.make_async_remote_copy(
            src_ref=res.at[c, d], dst_ref=out_ref.at[rows_of(d, c)],
            send_sem=bsend.at[c, d], recv_sem=brecv.at[c, d],
            device_id={"patch": zz, "tm": yy}, device_id_type=MESH)

    loads[0].wait()
    loads[1].wait()
    normed = layer_norm(x[...])
    packed[:, :width] = (dot(normed, sqkv[:, :width]).astype(bf16) * scale).astype(bf16)
    packed[:, width:] = dot(normed, sqkv[:, width:]).astype(bf16)
    loads[2].wait()
    pl.semaphore_wait(barrier, group - 1)

    for j in range(zs):
        zz = order[j * ys][0]
        rows = pl.ds(pl.multiple_of(zz * (ys * block), ys * block), ys * block)
        for p in range(pairs):
            lanes = slice(p * PAIR, (p + 1) * PAIR)
            attn[:, lanes] = attend(
                packed[rows, p * PAIR:(p + 1) * PAIR],
                packed[:, width + p * PAIR:width + (p + 1) * PAIR],
                packed[:, 2 * width + p * PAIR:2 * width + (p + 1) * PAIR], None)
        hid[rows, :] = (x[rows, :].astype(f32) + dot(attn[...], sout[...])).astype(bf16)
        for i in range(ys):
            zz, yy, d = order[j * ys + i]
            if j * ys + i < group - 1:
                forward(zz, yy, d, 0).start()
    for zz, yy, d in peers:
        for c in range(1, CHUNKS):
            forward(zz, yy, d, c).start()
    for c in range(CHUNKS):
        recv[c, pl.ds(me, 1)] = hid[rows_of(me, c), :].reshape(1, part, width)
    loads[3].wait()
    loads[4].wait()

    sub = 16
    keys = group * sub
    at_q = lax.broadcasted_iota(jnp.int32, (2 * keys, keys), 0) % keys
    at_k = lax.broadcasted_iota(jnp.int32, (2 * keys, keys), 1)
    allowed = (at_q % sub == at_k % sub) & (at_k // sub <= at_q // sub)
    for c in range(CHUNKS):
        for zz, yy, d in peers:
            forward_in(zz, yy, d, c).wait_recv()
        got = recv[c].reshape(group * part, width)
        normed = layer_norm(got)
        tpacked[:, :, :width] = (
            (dot(normed, tqkv[:, :width]).astype(bf16) * scale).astype(bf16).reshape(group, part, width))
        tpacked[:, :, width:] = (
            dot(normed, tqkv[:, width:]).astype(bf16).reshape(group, part, 2 * width))
        for s in range(part // sub):
            at = slice(s * sub, (s + 1) * sub)
            for p in range(pairs):
                lanes = slice(p * PAIR, (p + 1) * PAIR)
                q, k, v = (
                    tpacked[:, at, w * width + p * PAIR:w * width + (p + 1) * PAIR].reshape(keys, PAIR)
                    for w in range(3)
                )
                tattn[:, at, lanes] = attend(q, k, v, allowed).reshape(group, sub, PAIR)
        update = dot(tattn[...].reshape(group * part, width), tout[...])
        res[c] = (got.astype(f32) + update).astype(bf16).reshape(group, part, width)
        for zz, yy, d in peers:
            back(zz, yy, d, c).start()
        pltpu.make_async_copy(res.at[c, me], out_ref.at[rows_of(me, c)], own_sem.at[c]).start()

    for c in range(CHUNKS):
        for zz, yy, d in peers:
            forward(zz, yy, d, c).wait_send()
            back(zz, yy, d, c).wait_send()
            back_in(zz, yy, d, c).wait_recv()
        pltpu.make_async_copy(res.at[c, me], out_ref.at[rows_of(me, c)], own_sem.at[c]).wait()


def fused(zs, ys, frame, sqkv, sout, tqkv, tout):
    patches, width = frame.shape
    group = zs * ys
    block = patches // group
    part = block // CHUNKS
    anywhere = pl.BlockSpec(memory_space=pltpu.HBM)
    dma = pltpu.SemaphoreType.DMA
    return pl.pallas_call(
        functools.partial(fused_kernel, zs, ys),
        out_shape=jax.ShapeDtypeStruct((patches, width), bf16),
        in_specs=[anywhere] * 5,
        out_specs=anywhere,
        scratch_shapes=[
            pltpu.VMEM((patches, width), bf16),
            pltpu.VMEM(sqkv.shape, bf16),
            pltpu.VMEM(sout.shape, bf16),
            pltpu.VMEM(tqkv.shape, bf16),
            pltpu.VMEM(tout.shape, bf16),
            pltpu.VMEM((patches, 3 * width), bf16),
            pltpu.VMEM((patches, width), bf16),
            pltpu.VMEM((CHUNKS, group, part, width), bf16),
            pltpu.VMEM((group, part, 3 * width), bf16),
            pltpu.VMEM((ys * block, width), bf16),
            pltpu.VMEM((group, part, width), bf16),
            pltpu.VMEM((CHUNKS, group, part, width), bf16),
            dma((5,)),
            dma((CHUNKS,)),
            dma((CHUNKS, group)),
            dma((CHUNKS, group)),
            dma((CHUNKS, group)),
            dma((CHUNKS, group)),
        ],
        compiler_params=pltpu.CompilerParams(
            collective_id=0, has_side_effects=True, vmem_limit_bytes=62 * 2**20),
    )(frame, sqkv, sout, tqkv, tout)


def spatial_frame(one_frame, qkv_weight, out_weight):
    width = one_frame.shape[-1]
    scale = (width // HEADS) ** -0.5
    packed = dot(layer_norm(one_frame), qkv_weight).astype(bf16)
    queries, keys, values = jnp.split(packed, 3, axis=-1)
    queries = (queries * scale).astype(bf16)
    mixture = jnp.concatenate(
        [attend(queries[:, a:a + PAIR], keys[:, a:a + PAIR], values[:, a:a + PAIR], None)
         for a in range(0, width, PAIR)], axis=-1)
    return (one_frame.astype(f32) + dot(mixture, out_weight)).astype(bf16)


def temporal_columns(columns, qkv_weight, out_weight):
    frames, count, width = columns.shape
    scale = (width // HEADS) ** -0.5
    rows = columns.reshape(frames * count, width)
    packed = dot(layer_norm(rows), qkv_weight).astype(bf16)
    queries, keys, values = jnp.split(packed, 3, axis=-1)
    queries = (queries * scale).astype(bf16)
    place = jnp.arange(frames * count, dtype=jnp.int32)
    allowed = (place[:, None] % count == place[None, :] % count) & (
        place[None, :] // count <= place[:, None] // count)
    allowed = jnp.concatenate([allowed, allowed], axis=0)
    mixture = jnp.concatenate(
        [attend(queries[:, a:a + PAIR], keys[:, a:a + PAIR], values[:, a:a + PAIR], allowed)
         for a in range(0, width, PAIR)], axis=-1)
    return (rows.astype(f32) + dot(mixture, out_weight)).astype(bf16).reshape(columns.shape)


def solution(mesh):
    zs, ys = mesh.shape["patch"], mesh.shape["tm"]
    group = zs * ys

    def body(frames_in, spatial_qkv, spatial_out, temporal_qkv, temporal_out):
        frames, patches, width = frames_in.shape
        if frames == 1 and zs % 2 == 0 and patches % (16 * CHUNKS * group) == 0:
            return fused(zs, ys, frames_in[0], spatial_qkv, spatial_out, temporal_qkv, temporal_out)[None]
        hidden = lax.map(lambda frame: spatial_frame(frame, spatial_qkv, spatial_out), frames_in)
        columns = lax.all_to_all(hidden, ("patch", "tm"), split_axis=1, concat_axis=0, tiled=True)
        result = temporal_columns(columns, temporal_qkv, temporal_out)
        return lax.all_to_all(result, ("patch", "tm"), split_axis=0, concat_axis=1, tiled=True)

    in_specs = (P(("subject", "patch", "tm"), None, None), P(), P(), P(), P())
    out_specs = P(("subject", "patch", "tm"), None, None)
    return jax.shard_map(body, mesh=mesh, in_specs=in_specs, out_specs=out_specs, check_vma=False)
```
